32 devices in a mesh: seq: 16 (over z, x, core), dp: 2 (over y).
Axes of the slice: x: 2, y: 2, z: 4, core: 2. Of those that a mesh axis runs over, the one named last changes fastest.
Arguments:
- inputs: bfloat16 [2, 2048, 2048], P('dp', 'seq'), may hold values from -6 to 6
- filters: bfloat16 [2048, 2048], P('seq', 'dp'), may hold values from -6 to 6
- grad_out: bfloat16 [2, 2048, 2048], P('dp', 'seq'), may hold values from -0.125 to 0.125
Outputs:
- grad_inputs: bfloat16 [2, 2048, 2048], P('dp', 'seq')
- grad_filters: bfloat16 [2048, 2048], P('seq', 'dp')
The draws below stay inside these ranges and needn't reach their ends.
All inputs are finite; a program needn't handle non-finite values.
Results may differ from the reference program's by a relative error of at most 0.001.
Values may be sent and summed in bfloat16 or wider, within the bound.
A program may use at most 128 MiB of HBM per device.

```python
import jax
import jax.numpy as jnp

C = 2048
TOKENS = 2048
BATCH = 2


def steps_of(own_key, extent, pieces, least, largest):
    level = 1.0
    for position, parts in pieces:
        heights = jax.random.uniform(jax.random.fold_in(jax.random.fold_in(own_key, 6), position), (parts,), jnp.float32, least / len(pieces), largest / len(pieces))
        level = level * jnp.repeat(jnp.exp(heights), extent[position] // parts).reshape((-1,) + (1,) * (len(extent) - 1 - position))
    return level


def gaussian(key, shape, deviation, most, pieces=(), dtype=jnp.bfloat16):
    result = jax.random.normal(key, shape, jnp.float32) * deviation
    if len(pieces) > 0:
        result = steps_of(key, shape, pieces, -0.22, 0.18) * result
    return jnp.clip(result, min=-most, max=most).astype(dtype)


def setup_inputs(seed: int = 0) -> dict:
    arg_keys = jax.random.split(jax.random.key(seed), 4)
    inputs = gaussian(arg_keys[0], (BATCH, TOKENS, C), 1.0, 6.0, ((0, 2), (1, 16)))
    filters = gaussian(arg_keys[1], (TOKENS, C), 1.0, 6.0, ((0, 16), (1, 2)))
    grad_out = gaussian(arg_keys[2], (BATCH, TOKENS, C), TOKENS ** -0.5, 0.125, ((0, 2), (1, 16)))
    return dict(inputs=inputs, filters=filters, grad_out=grad_out)


def reference(inputs, filters, grad_out):
    length = 2 * TOKENS
    spectrum_in = jnp.fft.rfft(inputs.astype(jnp.float32), n=length, axis=1)
    spectrum_out = jnp.fft.rfft(grad_out.astype(jnp.float32), n=length, axis=1)
    spectrum_filter = jnp.fft.rfft(filters.astype(jnp.float32), n=length, axis=0)
    input_product = jnp.conj(spectrum_filter)[None] * spectrum_out
    grad_inputs = jnp.fft.irfft(input_product, n=length, axis=1)[:, :TOKENS]
    filter_product = jnp.sum(jnp.conj(spectrum_in) * spectrum_out, axis=0)
    grad_filters = jnp.fft.irfft(filter_product, n=length, axis=0)[:TOKENS]
    return grad_inputs.astype(jnp.bfloat16), grad_filters.astype(jnp.bfloat16)
```

```python
import functools
import math

import jax
import jax.numpy as jnp
import ml_dtypes
import numpy as np
from jax import lax
from jax.experimental import pallas as pl
from jax.experimental.pallas import tpu as pltpu
from jax.sharding import PartitionSpec as P

exact_mode = lax.Precision.HIGHEST


def phases(left_index, right_index, modulus):
    product = left_index[:, None] * right_index[None, :] % modulus
    angles = 2.0 * math.pi / modulus * product.astype(jnp.float32)
    return (jnp.cos(angles), jnp.sin(angles))


def across(block_in, length_all):
    seq_parts = block_in.shape[0]
    slot_rows = block_in.shape[1]
    values = block_in.astype(jnp.float32)
    cosine, sine_table = phases(
        jnp.arange(2 * seq_parts, dtype=jnp.int32),
        jnp.arange(seq_parts, dtype=jnp.int32),
        2 * seq_parts,
    )
    real_part = jnp.einsum("kp,pjw->kjw", cosine, values, precision=exact_mode)
    imag_part = -jnp.einsum("kp,pjw->kjw", sine_table, values, precision=exact_mode)
    twist_cos, twist_sin = phases(
        jnp.arange(2 * seq_parts, dtype=jnp.int32),
        jnp.arange(slot_rows, dtype=jnp.int32),
        length_all,
    )
    twist_cos = twist_cos[:, :, None]
    twist_sin = twist_sin[:, :, None]
    return jnp.stack(
        [
            real_part * twist_cos + imag_part * twist_sin,
            imag_part * twist_cos - real_part * twist_sin,
        ]
    )


def along(spectra):
    row_count = spectra.shape[2]
    index_rows = jnp.arange(row_count, dtype=jnp.int32)
    cosine, sine_table = phases(index_rows, index_rows, row_count)
    cos_real = jnp.einsum("kn,rnw->rkw", cosine, spectra[0], precision=exact_mode)
    cos_imag = jnp.einsum("kn,rnw->rkw", cosine, spectra[1], precision=exact_mode)
    sin_real = jnp.einsum("kn,rnw->rkw", sine_table, spectra[0], precision=exact_mode)
    sin_imag = jnp.einsum("kn,rnw->rkw", sine_table, spectra[1], precision=exact_mode)
    return jnp.stack([cos_real + sin_imag, cos_imag - sin_real])


def back_along(spectra, length_all):
    row_count = spectra.shape[2]
    coarse = spectra.shape[1]
    index_rows = jnp.arange(row_count, dtype=jnp.int32)
    cosine, sine_table = phases(index_rows, index_rows, row_count)
    cos_real = jnp.einsum("nk,rkw->rnw", cosine, spectra[0], precision=exact_mode)
    cos_imag = jnp.einsum("nk,rkw->rnw", cosine, spectra[1], precision=exact_mode)
    sin_real = jnp.einsum("nk,rkw->rnw", sine_table, spectra[0], precision=exact_mode)
    sin_imag = jnp.einsum("nk,rkw->rnw", sine_table, spectra[1], precision=exact_mode)
    inner_real = cos_real - sin_imag
    inner_imag = cos_imag + sin_real
    twist_cos, twist_sin = phases(jnp.arange(coarse, dtype=jnp.int32), index_rows, length_all)
    twist_cos = twist_cos[:, :, None]
    twist_sin = twist_sin[:, :, None]
    return jnp.stack(
        [
            inner_real * twist_cos - inner_imag * twist_sin,
            inner_imag * twist_cos + inner_real * twist_sin,
        ]
    )


def collapse(spectra, length_all):
    coarse = spectra.shape[1]
    seq_parts = coarse // 2
    cosine, sine_table = phases(
        jnp.arange(seq_parts, dtype=jnp.int32), jnp.arange(coarse, dtype=jnp.int32), coarse
    )
    values = jnp.einsum("nk,kjw->njw", cosine, spectra[0], precision=exact_mode)
    values = values - jnp.einsum("nk,kjw->njw", sine_table, spectra[1], precision=exact_mode)
    return values * (1.0 / length_all)


def paired(left_spec, right_spec):
    real_part = left_spec[0] * right_spec[0] + left_spec[1] * right_spec[1]
    imag_part = left_spec[0] * right_spec[1] - left_spec[1] * right_spec[0]
    return jnp.stack([real_part, imag_part])


def spread(matrix, dp_groups, seq_parts):
    row_count = matrix.shape[0]
    narrow = matrix.shape[1] // (dp_groups * seq_parts)
    return jnp.transpose(matrix.reshape(row_count, dp_groups, seq_parts, narrow), (0, 2, 1, 3))


def per_device(inputs, filters, grad_out):
    row_count = inputs.shape[1]
    channels = inputs.shape[2]
    seq_parts = lax.axis_size("seq")
    dp_groups = lax.axis_size("dp")
    length_all = 2 * seq_parts * row_count
    signal = inputs[0]
    cotangent = grad_out[0]
    whole_filter = lax.all_gather(filters, "dp", axis=1, tiled=True)
    narrow = channels // (dp_groups * seq_parts)
    stacked = jnp.stack(
        [
            spread(signal, dp_groups, seq_parts),
            spread(cotangent, dp_groups, seq_parts),
            spread(whole_filter, dp_groups, seq_parts),
        ],
        axis=2,
    )
    moved_rows = lax.all_to_all(stacked, "seq", split_axis=1, concat_axis=0, tiled=True)
    local_grid = moved_rows.reshape(seq_parts, row_count, 3 * dp_groups * narrow)
    spectra = along(across(local_grid, length_all))
    spectra = spectra.reshape(2, 2 * seq_parts, row_count, 3, dp_groups, narrow)
    input_spec = paired(spectra[:, :, :, 2], spectra[:, :, :, 1])
    filter_spec = paired(spectra[:, :, :, 0], spectra[:, :, :, 1])
    joined = jnp.concatenate([input_spec, filter_spec], axis=3)
    slot_count = joined.shape[3]
    flattened = joined.reshape(2, joined.shape[1], row_count, slot_count * narrow)
    result = collapse(back_along(flattened, length_all), length_all).reshape(
        seq_parts * row_count, slot_count, narrow
    )
    grad_in = result[:, :dp_groups]
    grad_filter = lax.psum_scatter(result[:, dp_groups:], "dp", scatter_dimension=1, tiled=True)
    outgoing = jnp.concatenate([grad_in, grad_filter], axis=1).astype(jnp.bfloat16)
    outgoing = outgoing.reshape(seq_parts * row_count, 1, dp_groups + 1, narrow)
    returned = lax.all_to_all(outgoing, "seq", split_axis=0, concat_axis=1, tiled=True)
    grad_inputs = jnp.transpose(returned[:, :, :dp_groups], (0, 2, 1, 3)).reshape(
        1, row_count, channels
    )
    grad_filters = returned[:, :, dp_groups].reshape(row_count, channels // dp_groups)
    return (grad_inputs, grad_filters)


lanes = 128
tile_rows = 16
f32 = jnp.float32
bf16 = jnp.bfloat16


def tables(parts, rows):
    total = 2 * parts * rows
    coarse = np.arange(parts + 1)[:, None, None]
    fine = np.arange(rows)[None, :, None]
    index = np.arange(rows)[None, None, :]
    angle = 2.0 * np.pi / total * (index * (coarse + 2 * parts * fine) % total)
    cosine, sine = np.cos(angle), np.sin(angle)
    forward = np.concatenate(
        [
            np.concatenate([cosine, sine], axis=2),
            np.concatenate([-sine, cosine], axis=2),
        ],
        axis=1,
    )
    weight = np.where((np.arange(parts + 1) % parts) == 0, 1.0, 2.0) / total
    backward = np.transpose(forward, (0, 2, 1)) * weight[:, None, None]

    def two_terms(matrix):
        high = matrix.astype(ml_dtypes.bfloat16)
        low = (matrix - high.astype(np.float64)).astype(ml_dtypes.bfloat16)
        return np.stack([high, low], axis=1)

    return two_terms(forward), two_terms(backward)


def spread_dft(values):
    count = len(values)
    if count == 1:
        return [(values[0], None), (values[0], None)]
    even, odd = spread_dft(values[0::2]), spread_dft(values[1::2])
    half = count // 2
    out = [None] * (count + 1)
    out[0] = (even[0][0] + odd[0][0], None)
    out[count] = (even[0][0] - odd[0][0], None)
    for k in range(1, half):
        c, s = math.cos(math.pi * k / count), math.sin(math.pi * k / count)
        real = odd[k][0] * c + odd[k][1] * s
        imag = odd[k][1] * c - odd[k][0] * s
        out[k] = (even[k][0] + real, even[k][1] + imag)
        out[count - k] = (even[k][0] - real, imag - even[k][1])
    out[half] = (even[half][0], -odd[half][0])
    return out


def gather_dft(spectrum):
    count = len(spectrum) - 1
    if count == 1:
        return [spectrum[0][0] + spectrum[1][0]]
    half = count // 2
    even, odd = [None] * (half + 1), [None] * (half + 1)
    even[0] = (spectrum[0][0] + spectrum[count][0], None)
    odd[0] = (spectrum[0][0] - spectrum[count][0], None)
    for k in range(1, half):
        c, s = math.cos(math.pi * k / count), math.sin(math.pi * k / count)
        ar, ai = spectrum[k]
        br, bi = spectrum[count - k]
        even[k] = (ar + br, ai - bi)
        dr, di = ar - br, ai + bi
        odd[k] = (dr * c - di * s, di * c + dr * s)
    even[half] = (spectrum[half][0], None)
    odd[half] = (-spectrum[half][1], None)
    out = [None] * count
    out[0::2] = gather_dft(even)
    out[1::2] = gather_dft(odd)
    return out


def two_terms_of(value):
    high = value.astype(bf16)
    return high, (value - high.astype(f32)).astype(bf16)


def exact_dot(table, k, high, low):
    dot = functools.partial(jnp.dot, preferred_element_type=f32)
    return dot(table[k, 0], high) + dot(table[k, 0], low) + dot(table[k, 1], high)


def kernel(
    parts,
    x_ref,
    g_ref,
    f_ref,
    fwd_hbm,
    inv_hbm,
    gi_ref,
    gf_ref,
    fwd,
    inv,
    xs,
    gs,
    fs,
    xr,
    gr,
    fr,
    gis,
    gfs,
    gir,
    gfr,
    fg_high,
    fg_low,
    x_high,
    x_low,
    g_spec,
    inner,
    table_sem,
    xs_sem,
    xr_sem,
    gs_sem,
    gr_sem,
    fs_sem,
    fr_sem,
    gis_sem,
    gir_sem,
    gfs_sem,
    gfr_sem,
):
    me_s, me_d = lax.axis_index("seq"), lax.axis_index("dp")
    everyone = 2 * parts
    me = me_s * 2 + me_d
    own = me_d * parts + me_s
    rows = x_ref.shape[0]
    half = rows // 2
    low_half = lax.broadcasted_iota(jnp.int32, (half, lanes), 1) < lanes // 2
    low_tile = lax.broadcasted_iota(jnp.int32, (tile_rows, lanes), 1) < lanes // 2

    def swap(mask, first, second):
        return (
            jnp.where(mask, first, pltpu.roll(second, lanes // 2, 1)),
            jnp.where(mask, pltpu.roll(first, lanes // 2, 1), second),
        )

    def loop(start, stop, body):
        def step(i, carry):
            body(i)
            return carry

        lax.fori_loop(start, stop, step, 0)

    def partner(o):
        other = lax.rem(me + o, everyone)
        return lax.div(other, 2), lax.rem(other, 2)

    def peer(o):
        return lax.rem(me_s + o, parts)

    barrier = pltpu.get_barrier_semaphore()

    def greet(o):
        s, d = partner(o)
        pl.semaphore_signal(
            barrier, inc=1, device_id=(s, d), device_id_type=pl.DeviceIdType.MESH
        )

    loop(1, everyone, greet)
    fwd_copy = pltpu.make_async_copy(fwd_hbm, fwd, table_sem.at[0])
    inv_copy = pltpu.make_async_copy(inv_hbm, inv, table_sem.at[1])
    fwd_copy.start()
    inv_copy.start()

    def pack(source, target):
        def step(m):
            column = pl.ds(pl.multiple_of(m * lanes, lanes), lanes)
            first, second = swap(
                low_half,
                source[0:half, column].astype(f32),
                source[half:rows, column].astype(f32),
            )
            target[2 * m] = first.astype(bf16)
            target[2 * m + 1] = second.astype(bf16)

        loop(0, source.shape[1] // lanes, step)

    def unpack(source, target):
        def step(m):
            column = pl.ds(pl.multiple_of(m * lanes, lanes), lanes)
            first, second = swap(
                low_half, source[2 * m].astype(f32), source[2 * m + 1].astype(f32)
            )
            target[0:half, column] = first.astype(bf16)
            target[half:rows, column] = second.astype(bf16)

        loop(0, target.shape[1] // lanes, step)

    def to_all(source, target, send, receive):
        def copy(o):
            s, d = partner(o)
            return pltpu.make_async_remote_copy(
                src_ref=source.at[d * parts + s],
                dst_ref=target.at[own],
                send_sem=send.at[d * parts + s],
                recv_sem=receive.at[own],
                device_id=(s, d),
                device_id_type=pl.DeviceIdType.MESH,
            )

        def arrived(o):
            s, d = partner(o)
            pltpu.make_async_remote_copy(
                src_ref=source.at[own],
                dst_ref=target.at[d * parts + s],
                send_sem=send.at[own],
                recv_sem=receive.at[d * parts + s],
                device_id=(s, d),
                device_id_type=pl.DeviceIdType.MESH,
            ).wait_recv()

        def start():
            loop(1, everyone, lambda o: copy(o).start())
            target[own] = source[own]

        def wait():
            loop(1, everyone, arrived)

        def sent():
            loop(1, everyone, lambda o: copy(o).wait_send())

        return start, wait, sent

    def to_row(source, target, send, receive):
        def copy(o):
            return pltpu.make_async_remote_copy(
                src_ref=source.at[peer(o)],
                dst_ref=target.at[me_s],
                send_sem=send.at[peer(o)],
                recv_sem=receive.at[me_s],
                device_id=(peer(o), me_d),
                device_id_type=pl.DeviceIdType.MESH,
            )

        def arrived(o):
            pltpu.make_async_remote_copy(
                src_ref=source.at[me_s],
                dst_ref=target.at[peer(o)],
                send_sem=send.at[me_s],
                recv_sem=receive.at[peer(o)],
                device_id=(peer(o), me_d),
                device_id_type=pl.DeviceIdType.MESH,
            ).wait_recv()

        def start():
            loop(1, parts, lambda o: copy(o).start())
            target[me_s] = source[me_s]

        def wait():
            loop(1, parts, arrived)

        def sent():
            loop(1, parts, lambda o: copy(o).wait_send())

        return start, wait, sent

    f_start, f_wait, f_sent = to_row(fs, fr, fs_sem, fr_sem)
    g_start, g_wait, g_sent = to_all(gs, gr, gs_sem, gr_sem)
    x_start, x_wait, x_sent = to_all(xs, xr, xs_sem, xr_sem)
    gi_start, gi_wait, gi_sent = to_all(gis, gir, gis_sem, gir_sem)
    gf_start, gf_wait, gf_sent = to_row(gfs, gfr, gfs_sem, gfr_sem)

    pack(f_ref, fs)
    pack(g_ref, gs)
    pl.semaphore_wait(barrier, everyone - 1)
    f_start()
    g_start()
    pack(x_ref, xs)
    x_start()

    zeros = jnp.zeros((rows, lanes), bf16)

    def spread_to(load, high, low, lane_at):
        columns = slice(lane_at, lane_at + lanes)
        for k in (0, parts):
            high[k, rows:, columns] = zeros
            low[k, rows:, columns] = zeros

        def step(t):
            at = pl.multiple_of(t * tile_rows, tile_rows)
            for side in range(2):
                values = [load(p, pl.ds(at, tile_rows))[side] for p in range(parts)]
                for k, (real, imag) in enumerate(spread_dft(values)):
                    where = pl.ds(side * half + at, tile_rows)
                    high[k, where, columns], low[k, where, columns] = two_terms_of(real)
                    if imag is not None:
                        where = pl.ds(rows + side * half + at, tile_rows)
                        high[k, where, columns], low[k, where, columns] = two_terms_of(imag)

        loop(0, half // tile_rows, step)

    def load_pair(source):
        def load(p, where):
            return swap(
                low_tile, source[p, where].astype(f32), source[parts + p, where].astype(f32)
            )

        return load

    def load_twice(p, where):
        value = fr[p, where].astype(f32)
        return swap(low_tile, value, value)

    def product(left, right):
        lr, li, rr, ri = left[:rows], left[rows:], right[:rows], right[rows:]
        return two_terms_of(
            jnp.concatenate([lr * rr + li * ri, lr * ri - li * rr], axis=0)
        )

    def gather_from(store):
        def step(t):
            at = pl.multiple_of(t * tile_rows, tile_rows)
            found = []
            for side in range(2):
                spectrum = []
                for k in range(parts + 1):
                    real = inner[k, pl.ds(side * half + at, tile_rows)]
                    imag = None
                    if k % parts:
                        imag = inner[k, pl.ds(rows + side * half + at, tile_rows)]
                    spectrum.append((real, imag))
                found.append(gather_dft(spectrum))
            for q in range(parts):
                store(q, pl.ds(at, tile_rows), found[0][q], found[1][q])

        loop(0, half // tile_rows, step)

    f_wait()
    spread_to(load_twice, fg_high, fg_low, 0)
    g_wait()
    spread_to(load_pair(gr), fg_high, fg_low, lanes)
    fwd_copy.wait()
    inv_copy.wait()

    def input_step(k):
        both = exact_dot(fwd, k, fg_high[k], fg_low[k])
        right = both[:, lanes:]
        g_spec[k] = right
        inner[k] = exact_dot(inv, k, *product(both[:, :lanes], right))

    loop(0, parts + 1, input_step)

    def store_input(q, where, top, bottom):
        first, second = swap(low_tile, top, bottom)
        gis[q, where] = first.astype(bf16)
        gis[parts + q, where] = second.astype(bf16)

    gather_from(store_input)
    gi_start()

    x_wait()
    spread_to(load_pair(xr), x_high, x_low, 0)

    def filter_step(k):
        left = exact_dot(fwd, k, x_high[k], x_low[k])
        inner[k] = exact_dot(inv, k, *product(left, g_spec[k]))

    loop(0, parts + 1, filter_step)

    def store_filter(q, where, top, bottom):
        first, second = swap(low_tile, top, bottom)
        gfs[q, where] = (first + second).astype(bf16)

    gather_from(store_filter)
    gf_start()

    gi_wait()
    unpack(gir, gi_ref)
    gf_wait()
    unpack(gfr, gf_ref)
    for sent in (f_sent, g_sent, x_sent, gi_sent, gf_sent):
        sent()


def whole_kernel(inputs, filters, grad_out):
    rows, channels = inputs.shape[1], inputs.shape[2]
    parts = lax.axis_size("seq")
    forward, backward = tables(parts, rows)
    half = rows // 2
    every = lambda: pltpu.VMEM((2 * parts, half, lanes), bf16)
    row = lambda: pltpu.VMEM((parts, half, lanes), bf16)
    spec = lambda width, dtype: pltpu.VMEM((parts + 1, 2 * rows, width), dtype)
    sems = lambda count: pltpu.SemaphoreType.DMA((count,))
    vmem = pl.BlockSpec(memory_space=pltpu.VMEM)
    hbm = pl.BlockSpec(memory_space=pl.ANY)
    grad_in, grad_filter = pl.pallas_call(
        functools.partial(kernel, parts),
        out_shape=(
            jax.ShapeDtypeStruct((rows, channels), bf16),
            jax.ShapeDtypeStruct(filters.shape, bf16),
        ),
        in_specs=[vmem, vmem, vmem, hbm, hbm],
        out_specs=(vmem, vmem),
        scratch_shapes=[
            pltpu.VMEM(forward.shape, bf16),
            pltpu.VMEM(backward.shape, bf16),
            every(),
            every(),
            row(),
            every(),
            every(),
            row(),
            every(),
            row(),
            every(),
            row(),
            spec(2 * lanes, bf16),
            spec(2 * lanes, bf16),
            spec(lanes, bf16),
            spec(lanes, bf16),
            spec(lanes, f32),
            spec(lanes, f32),
            sems(2),
            sems(2 * parts),
            sems(2 * parts),
            sems(2 * parts),
            sems(2 * parts),
            sems(parts),
            sems(parts),
            sems(2 * parts),
            sems(2 * parts),
            sems(parts),
            sems(parts),
        ],
        compiler_params=pltpu.CompilerParams(
            collective_id=0, has_side_effects=True, vmem_limit_bytes=50 * 2**20
        ),
    )(inputs[0], grad_out[0], filters, jnp.asarray(forward), jnp.asarray(backward))
    return grad_in[None], grad_filter


def choose(inputs, filters, grad_out):
    rows, channels = inputs.shape[1], inputs.shape[2]
    parts, groups = lax.axis_size("seq"), lax.axis_size("dp")
    fits = (
        groups == 2
        and channels == lanes // 2 * groups * parts
        and rows % (2 * tile_rows) == 0
        and parts % 2 == 0
        and parts <= 16
        and rows <= 128
    )
    return (whole_kernel if fits else per_device)(inputs, filters, grad_out)


def solution(mesh):
    return jax.shard_map(
        choose,
        mesh=mesh,
        in_specs=(P("dp", "seq", None), P("seq", "dp"), P("dp", "seq", None)),
        out_specs=(P("dp", "seq", None), P("seq", "dp")),
        check_vma=False,
    )
```

```python
import functools
import math

import jax
import jax.numpy as jnp
import ml_dtypes
import numpy as np
from jax import lax
from jax.experimental import pallas as pl
from jax.experimental.pallas import tpu as pltpu
from jax.sharding import PartitionSpec as P

exact_mode = lax.Precision.HIGHEST


def phases(left_index, right_index, modulus):
    product = left_index[:, None] * right_index[None, :] % modulus
    angles = 2.0 * math.pi / modulus * product.astype(jnp.float32)
    return (jnp.cos(angles), jnp.sin(angles))


def across(block_in, length_all):
    seq_parts = block_in.shape[0]
    slot_rows = block_in.shape[1]
    values = block_in.astype(jnp.float32)
    cosine, sine_table = phases(
        jnp.arange(2 * seq_parts, dtype=jnp.int32),
        jnp.arange(seq_parts, dtype=jnp.int32),
        2 * seq_parts,
    )
    real_part = jnp.einsum("kp,pjw->kjw", cosine, values, precision=exact_mode)
    imag_part = -jnp.einsum("kp,pjw->kjw", sine_table, values, precision=exact_mode)
    twist_cos, twist_sin = phases(
        jnp.arange(2 * seq_parts, dtype=jnp.int32),
        jnp.arange(slot_rows, dtype=jnp.int32),
        length_all,
    )
    twist_cos = twist_cos[:, :, None]
    twist_sin = twist_sin[:, :, None]
    return jnp.stack(
        [
            real_part * twist_cos + imag_part * twist_sin,
            imag_part * twist_cos - real_part * twist_sin,
        ]
    )


def along(spectra):
    row_count = spectra.shape[2]
    index_rows = jnp.arange(row_count, dtype=jnp.int32)
    cosine, sine_table = phases(index_rows, index_rows, row_count)
    cos_real = jnp.einsum("kn,rnw->rkw", cosine, spectra[0], precision=exact_mode)
    cos_imag = jnp.einsum("kn,rnw->rkw", cosine, spectra[1], precision=exact_mode)
    sin_real = jnp.einsum("kn,rnw->rkw", sine_table, spectra[0], precision=exact_mode)
    sin_imag = jnp.einsum("kn,rnw->rkw", sine_table, spectra[1], precision=exact_mode)
    return jnp.stack([cos_real + sin_imag, cos_imag - sin_real])


def back_along(spectra, length_all):
    row_count = spectra.shape[2]
    coarse = spectra.shape[1]
    index_rows = jnp.arange(row_count, dtype=jnp.int32)
    cosine, sine_table = phases(index_rows, index_rows, row_count)
    cos_real = jnp.einsum("nk,rkw->rnw", cosine, spectra[0], precision=exact_mode)
    cos_imag = jnp.einsum("nk,rkw->rnw", cosine, spectra[1], precision=exact_mode)
    sin_real = jnp.einsum("nk,rkw->rnw", sine_table, spectra[0], precision=exact_mode)
    sin_imag = jnp.einsum("nk,rkw->rnw", sine_table, spectra[1], precision=exact_mode)
    inner_real = cos_real - sin_imag
    inner_imag = cos_imag + sin_real
    twist_cos, twist_sin = phases(jnp.arange(coarse, dtype=jnp.int32), index_rows, length_all)
    twist_cos = twist_cos[:, :, None]
    twist_sin = twist_sin[:, :, None]
    return jnp.stack(
        [
            inner_real * twist_cos - inner_imag * twist_sin,
            inner_imag * twist_cos + inner_real * twist_sin,
        ]
    )


def collapse(spectra, length_all):
    coarse = spectra.shape[1]
    seq_parts = coarse // 2
    cosine, sine_table = phases(
        jnp.arange(seq_parts, dtype=jnp.int32), jnp.arange(coarse, dtype=jnp.int32), coarse
    )
    values = jnp.einsum("nk,kjw->njw", cosine, spectra[0], precision=exact_mode)
    values = values - jnp.einsum("nk,kjw->njw", sine_table, spectra[1], precision=exact_mode)
    return values * (1.0 / length_all)


def paired(left_spec, right_spec):
    real_part = left_spec[0] * right_spec[0] + left_spec[1] * right_spec[1]
    imag_part = left_spec[0] * right_spec[1] - left_spec[1] * right_spec[0]
    return jnp.stack([real_part, imag_part])


def spread(matrix, dp_groups, seq_parts):
    row_count = matrix.shape[0]
    narrow = matrix.shape[1] // (dp_groups * seq_parts)
    return jnp.transpose(matrix.reshape(row_count, dp_groups, seq_parts, narrow), (0, 2, 1, 3))


def per_device(inputs, filters, grad_out):
    row_count = inputs.shape[1]
    channels = inputs.shape[2]
    seq_parts = lax.axis_size("seq")
    dp_groups = lax.axis_size("dp")
    length_all = 2 * seq_parts * row_count
    signal = inputs[0]
    cotangent = grad_out[0]
    whole_filter = lax.all_gather(filters, "dp", axis=1, tiled=True)
    narrow = channels // (dp_groups * seq_parts)
    stacked = jnp.stack(
        [
            spread(signal, dp_groups, seq_parts),
            spread(cotangent, dp_groups, seq_parts),
            spread(whole_filter, dp_groups, seq_parts),
        ],
        axis=2,
    )
    moved_rows = lax.all_to_all(stacked, "seq", split_axis=1, concat_axis=0, tiled=True)
    local_grid = moved_rows.reshape(seq_parts, row_count, 3 * dp_groups * narrow)
    spectra = along(across(local_grid, length_all))
    spectra = spectra.reshape(2, 2 * seq_parts, row_count, 3, dp_groups, narrow)
    input_spec = paired(spectra[:, :, :, 2], spectra[:, :, :, 1])
    filter_spec = paired(spectra[:, :, :, 0], spectra[:, :, :, 1])
    joined = jnp.concatenate([input_spec, filter_spec], axis=3)
    slot_count = joined.shape[3]
    flattened = joined.reshape(2, joined.shape[1], row_count, slot_count * narrow)
    result = collapse(back_along(flattened, length_all), length_all).reshape(
        seq_parts * row_count, slot_count, narrow
    )
    grad_in = result[:, :dp_groups]
    grad_filter = lax.psum_scatter(result[:, dp_groups:], "dp", scatter_dimension=1, tiled=True)
    outgoing = jnp.concatenate([grad_in, grad_filter], axis=1).astype(jnp.bfloat16)
    outgoing = outgoing.reshape(seq_parts * row_count, 1, dp_groups + 1, narrow)
    returned = lax.all_to_all(outgoing, "seq", split_axis=0, concat_axis=1, tiled=True)
    grad_inputs = jnp.transpose(returned[:, :, :dp_groups], (0, 2, 1, 3)).reshape(
        1, row_count, channels
    )
    grad_filters = returned[:, :, dp_groups].reshape(row_count, channels // dp_groups)
    return (grad_inputs, grad_filters)


lanes = 128
tile_rows = 16
group = 4
f32 = jnp.float32
bf16 = jnp.bfloat16


def tables(parts, rows):
    total = 2 * parts * rows
    coarse = np.arange(parts + 1)[:, None, None]
    fine = np.arange(rows)[None, :, None]
    index = np.arange(rows)[None, None, :]
    angle = 2.0 * np.pi / total * (index * (coarse + 2 * parts * fine) % total)
    cosine, sine = np.cos(angle), np.sin(angle)
    forward = np.concatenate(
        [
            np.concatenate([cosine, sine], axis=2),
            np.concatenate([-sine, cosine], axis=2),
        ],
        axis=1,
    )
    weight = np.where((np.arange(parts + 1) % parts) == 0, 1.0, 2.0) / total
    backward = np.transpose(forward, (0, 2, 1)) * weight[:, None, None]

    def two_terms(matrix):
        high = matrix.astype(ml_dtypes.bfloat16)
        low = (matrix - high.astype(np.float64)).astype(ml_dtypes.bfloat16)
        return np.concatenate([high, low], axis=1)

    return two_terms(forward), two_terms(backward)


def spread_dft(values):
    count = len(values)
    if count == 1:
        return [(values[0], None), (values[0], None)]
    even, odd = spread_dft(values[0::2]), spread_dft(values[1::2])
    half = count // 2
    out = [None] * (count + 1)
    out[0] = (even[0][0] + odd[0][0], None)
    out[count] = (even[0][0] - odd[0][0], None)
    for k in range(1, half):
        c, s = math.cos(math.pi * k / count), math.sin(math.pi * k / count)
        real = odd[k][0] * c + odd[k][1] * s
        imag = odd[k][1] * c - odd[k][0] * s
        out[k] = (even[k][0] + real, even[k][1] + imag)
        out[count - k] = (even[k][0] - real, imag - even[k][1])
    out[half] = (even[half][0], -odd[half][0])
    return out


def gather_dft(spectrum):
    count = len(spectrum) - 1
    if count == 1:
        return [spectrum[0][0] + spectrum[1][0]]
    half = count // 2
    even, odd = [None] * (half + 1), [None] * (half + 1)
    even[0] = (spectrum[0][0] + spectrum[count][0], None)
    odd[0] = (spectrum[0][0] - spectrum[count][0], None)
    for k in range(1, half):
        c, s = math.cos(math.pi * k / count), math.sin(math.pi * k / count)
        ar, ai = spectrum[k]
        br, bi = spectrum[count - k]
        even[k] = (ar + br, ai - bi)
        dr, di = ar - br, ai + bi
        odd[k] = (dr * c - di * s, di * c + dr * s)
    even[half] = (spectrum[half][0], None)
    odd[half] = (-spectrum[half][1], None)
    out = [None] * count
    out[0::2] = gather_dft(even)
    out[1::2] = gather_dft(odd)
    return out


def two_terms_of(value):
    high = value.astype(bf16)
    return high, (value - high.astype(f32)).astype(bf16)


def exact_dot(table, k, high, low):
    dot = functools.partial(jnp.dot, preferred_element_type=f32)
    size = table.shape[2]
    if high.shape[1] == lanes:
        four = dot(table[k], jnp.concatenate([high, low], axis=1))
        return four[:size, :lanes] + (four[:size, lanes:] + four[size:, :lanes])
    two = dot(table[k], high)
    return two[:size] + (two[size:] + dot(table[k, :size], low))


def kernel(
    parts,
    x_hbm,
    g_hbm,
    f_hbm,
    fwd_hbm,
    inv_hbm,
    gi_hbm,
    gf_hbm,
    gi_ref,
    gf_ref,
    x_ref,
    g_ref,
    f_ref,
    fwd,
    inv,
    xs,
    gs,
    fs,
    xr,
    gr,
    fr,
    gis,
    gfs,
    gir,
    gfr,
    fg_high,
    fg_low,
    x_high,
    x_low,
    g_spec,
    inner,
    table_sem,
    xs_sem,
    xr_sem,
    gs_sem,
    gr_sem,
    fs_sem,
    fr_sem,
    gis_sem,
    gir_sem,
    gfs_sem,
    gfr_sem,
):
    me_s, me_d = lax.axis_index("seq"), lax.axis_index("dp")
    everyone = 2 * parts
    me = me_s * 2 + me_d
    own = me_d * parts + me_s
    rows = x_ref.shape[0]
    half = rows // 2
    low_half = lax.broadcasted_iota(jnp.int32, (half, lanes), 1) < lanes // 2
    low_tile = lax.broadcasted_iota(jnp.int32, (tile_rows, lanes), 1) < lanes // 2

    def swap(mask, first, second):
        return (
            jnp.where(mask, first, pltpu.roll(second, lanes // 2, 1)),
            jnp.where(mask, pltpu.roll(first, lanes // 2, 1), second),
        )

    def loop(start, stop, body):
        def step(i, carry):
            body(i)
            return carry

        lax.fori_loop(start, stop, step, 0)

    def partner(o):
        other = lax.rem(me + o, everyone)
        return lax.div(other, 2), lax.rem(other, 2)

    barrier = pltpu.get_barrier_semaphore()

    def greet(o):
        s, d = partner(o)
        pl.semaphore_signal(
            barrier, inc=1, device_id=(s, d), device_id_type=pl.DeviceIdType.MESH
        )

    f_copy = pltpu.make_async_copy(f_hbm, f_ref, table_sem.at[2])
    g_copy = pltpu.make_async_copy(g_hbm, g_ref, table_sem.at[3])
    x_copy = pltpu.make_async_copy(x_hbm, x_ref, table_sem.at[4])
    fwd_copy = pltpu.make_async_copy(fwd_hbm, fwd, table_sem.at[0])
    inv_copy = pltpu.make_async_copy(inv_hbm, inv, table_sem.at[1])
    f_copy.start()
    g_copy.start()
    x_copy.start()
    loop(1, everyone, greet)
    fwd_copy.start()
    inv_copy.start()

    def pack(source, target, m):
        column = pl.ds(pl.multiple_of(m * lanes, lanes), lanes)
        first, second = swap(
            low_half,
            source[0:half, column].astype(f32),
            source[half:rows, column].astype(f32),
        )
        target[2 * m] = first.astype(bf16)
        target[2 * m + 1] = second.astype(bf16)

    def unpack(source, target):
        def step(m):
            column = pl.ds(pl.multiple_of(m * lanes, lanes), lanes)
            first, second = swap(
                low_half, source[2 * m].astype(f32), source[2 * m + 1].astype(f32)
            )
            target[0:half, column] = first.astype(bf16)
            target[half:rows, column] = second.astype(bf16)

        loop(0, target.shape[1] // lanes, step)

    def exchange(source, target, send, receive, mine, device_of):
        count = source.shape[0]

        def start(i):
            pltpu.make_async_remote_copy(
                src_ref=source.at[i],
                dst_ref=target.at[mine],
                send_sem=send.at[0],
                recv_sem=receive.at[0],
                device_id=device_of(i),
                device_id_type=pl.DeviceIdType.MESH,
            ).start()

        def pair(step, before):
            m = lax.rem(lax.div(mine, 2) + step, count // 2)
            if before is not None:
                before(m)
            for i in (2 * m, 2 * m + 1):
                pl.when(i != mine)(functools.partial(start, i))

        def start_all(before=None):
            loop(0, count // 2, lambda step: pair(step, before))
            target[mine] = source[mine]

        others = pl.ds(0, count - 1)
        everything = pltpu.make_async_remote_copy(
            src_ref=source.at[others],
            dst_ref=target.at[others],
            send_sem=send.at[0],
            recv_sem=receive.at[0],
            device_id=device_of(lax.rem(mine + 1, count)),
            device_id_type=pl.DeviceIdType.MESH,
        )
        return start_all, everything.wait_recv, everything.wait_send

    def to_all(*refs):
        return exchange(*refs, own, lambda i: (lax.rem(i, parts), lax.div(i, parts)))

    def to_row(*refs):
        return exchange(*refs, me_s, lambda i: (i, me_d))

    f_start, f_wait, f_sent = to_row(fs, fr, fs_sem, fr_sem)
    g_start, g_wait, g_sent = to_all(gs, gr, gs_sem, gr_sem)
    x_start, x_wait, x_sent = to_all(xs, xr, xs_sem, xr_sem)
    gi_start, gi_wait, gi_sent = to_all(gis, gir, gis_sem, gir_sem)
    gf_start, gf_wait, gf_sent = to_row(gfs, gfr, gfs_sem, gfr_sem)

    f_copy.wait()
    g_copy.wait()
    pl.semaphore_wait(barrier, everyone - 1)
    f_start(lambda m: pack(f_ref, fs, m))
    g_start(lambda m: pack(g_ref, gs, m))
    x_copy.wait()
    x_start(lambda m: pack(x_ref, xs, m))

    zeros = jnp.zeros((rows, lanes), bf16)

    def spread_to(load, high, low, lane_at):
        columns = slice(lane_at, lane_at + lanes)
        for k in (0, parts):
            high[k, rows:, columns] = zeros
            low[k, rows:, columns] = zeros

        def step(t):
            at = pl.multiple_of(t * tile_rows, tile_rows)
            for side in range(2):
                values = [load(p, pl.ds(at, tile_rows))[side] for p in range(parts)]
                for k, (real, imag) in enumerate(spread_dft(values)):
                    where = pl.ds(side * half + at, tile_rows)
                    high[k, where, columns], low[k, where, columns] = two_terms_of(real)
                    if imag is not None:
                        where = pl.ds(rows + side * half + at, tile_rows)
                        high[k, where, columns], low[k, where, columns] = two_terms_of(imag)

        loop(0, half // tile_rows, step)

    def load_pair(source):
        def load(p, where):
            return swap(
                low_tile, source[p, where].astype(f32), source[parts + p, where].astype(f32)
            )

        return load

    def load_twice(p, where):
        value = fr[p, where].astype(f32)
        return swap(low_tile, value, value)

    def product(left, right):
        lr, li, rr, ri = left[:rows], left[rows:], right[:rows], right[rows:]
        return two_terms_of(
            jnp.concatenate([lr * rr + li * ri, lr * ri - li * rr], axis=0)
        )

    def in_groups(step):
        loop(0, parts // group, lambda g: step([g * group + j for j in range(group)]))
        step([parts])

    def gather_from(store):
        def step(t):
            at = pl.multiple_of(t * tile_rows, tile_rows)
            found = []
            for side in range(2):
                spectrum = []
                for k in range(parts + 1):
                    real = inner[k, pl.ds(side * half + at, tile_rows)]
                    imag = None
                    if k % parts:
                        imag = inner[k, pl.ds(rows + side * half + at, tile_rows)]
                    spectrum.append((real, imag))
                found.append(gather_dft(spectrum))
            for q in range(parts):
                store(q, pl.ds(at, tile_rows), found[0][q], found[1][q])

        loop(0, half // tile_rows, step)

    f_wait()
    spread_to(load_twice, fg_high, fg_low, 0)
    g_wait()
    spread_to(load_pair(gr), fg_high, fg_low, lanes)
    fwd_copy.wait()
    inv_copy.wait()

    def input_step(ks):
        both = [exact_dot(fwd, k, fg_high[k], fg_low[k]) for k in ks]
        for k, spectrum in zip(ks, both):
            g_spec[k] = spectrum[:, lanes:]
        terms = [product(spectrum[:, :lanes], spectrum[:, lanes:]) for spectrum in both]
        for k, term in zip(ks, terms):
            inner[k] = exact_dot(inv, k, *term)

    in_groups(input_step)

    def store_input(q, where, top, bottom):
        first, second = swap(low_tile, top, bottom)
        gis[q, where] = first.astype(bf16)
        gis[parts + q, where] = second.astype(bf16)

    gather_from(store_input)
    gi_start()

    x_wait()
    spread_to(load_pair(xr), x_high, x_low, 0)

    def filter_step(ks):
        left = [exact_dot(fwd, k, x_high[k], x_low[k]) for k in ks]
        terms = [product(spectrum, g_spec[k]) for k, spectrum in zip(ks, left)]
        for k, term in zip(ks, terms):
            inner[k] = exact_dot(inv, k, *term)

    in_groups(filter_step)

    def store_filter(q, where, top, bottom):
        first, second = swap(low_tile, top, bottom)
        gfs[q, where] = (first + second).astype(bf16)

    gather_from(store_filter)
    gf_start()

    f_sent()
    g_sent()
    x_sent()
    gi_wait()
    unpack(gir, gi_ref)
    gi_copy = pltpu.make_async_copy(gi_ref, gi_hbm, table_sem.at[5])
    gi_copy.start()
    gi_sent()
    gf_wait()
    unpack(gfr, gf_ref)
    gf_copy = pltpu.make_async_copy(gf_ref, gf_hbm, table_sem.at[6])
    gf_copy.start()
    gf_sent()
    gi_copy.wait()
    gf_copy.wait()


def whole_kernel(inputs, filters, grad_out):
    rows, channels = inputs.shape[1], inputs.shape[2]
    parts = lax.axis_size("seq")
    forward, backward = tables(parts, rows)
    half = rows // 2
    every = lambda: pltpu.VMEM((2 * parts, half, lanes), bf16)
    row = lambda: pltpu.VMEM((parts, half, lanes), bf16)
    spec = lambda width, dtype: pltpu.VMEM((parts + 1, 2 * rows, width), dtype)
    sems = lambda count: pltpu.SemaphoreType.DMA((count,))
    hbm = pl.BlockSpec(memory_space=pltpu.HBM)
    grad_in, grad_filter = pl.pallas_call(
        functools.partial(kernel, parts),
        out_shape=(
            jax.ShapeDtypeStruct((rows, channels), bf16),
            jax.ShapeDtypeStruct(filters.shape, bf16),
        ),
        in_specs=[hbm] * 5,
        out_specs=(hbm, hbm),
        scratch_shapes=[
            pltpu.VMEM((rows, channels), bf16),
            pltpu.VMEM(filters.shape, bf16),
            pltpu.VMEM((rows, channels), bf16),
            pltpu.VMEM((rows, channels), bf16),
            pltpu.VMEM(filters.shape, bf16),
            pltpu.VMEM(forward.shape, bf16),
            pltpu.VMEM(backward.shape, bf16),
            every(),
            every(),
            row(),
            every(),
            every(),
            row(),
            every(),
            row(),
            every(),
            row(),
            spec(2 * lanes, bf16),
            spec(2 * lanes, bf16),
            spec(lanes, bf16),
            spec(lanes, bf16),
            spec(lanes, f32),
            spec(lanes, f32),
            sems(7),
            *[sems(1) for _ in range(10)],
        ],
        compiler_params=pltpu.CompilerParams(
            collective_id=0, has_side_effects=True, vmem_limit_bytes=60 * 2**20
        ),
    )(inputs[0], grad_out[0], filters, jnp.asarray(forward), jnp.asarray(backward))
    return grad_in[None], grad_filter


def choose(inputs, filters, grad_out):
    rows, channels = inputs.shape[1], inputs.shape[2]
    parts, groups = lax.axis_size("seq"), lax.axis_size("dp")
    fits = (
        groups == 2
        and channels == lanes // 2 * groups * parts
        and rows % (2 * tile_rows) == 0
        and parts % group == 0
        and parts <= 16
        and rows <= 128
    )
    return (whole_kernel if fits else per_device)(inputs, filters, grad_out)


def solution(mesh):
    return jax.shard_map(
        choose,
        mesh=mesh,
        in_specs=(P("dp", "seq", None), P("seq", "dp"), P("dp", "seq", None)),
        out_specs=(P("dp", "seq", None), P("seq", "dp")),
        check_vma=False,
    )
```

```python
import functools
import math

import jax
import jax.numpy as jnp
import ml_dtypes
import numpy as np
from jax import lax
from jax.experimental import pallas as pl
from jax.experimental.pallas import tpu as pltpu
from jax.sharding import PartitionSpec as P

exact_mode = lax.Precision.HIGHEST


def phases(left_index, right_index, modulus):
    product = left_index[:, None] * right_index[None, :] % modulus
    angles = 2.0 * math.pi / modulus * product.astype(jnp.float32)
    return (jnp.cos(angles), jnp.sin(angles))


def across(block_in, length_all):
    seq_parts = block_in.shape[0]
    slot_rows = block_in.shape[1]
    values = block_in.astype(jnp.float32)
    cosine, sine_table = phases(
        jnp.arange(2 * seq_parts, dtype=jnp.int32),
        jnp.arange(seq_parts, dtype=jnp.int32),
        2 * seq_parts,
    )
    real_part = jnp.einsum("kp,pjw->kjw", cosine, values, precision=exact_mode)
    imag_part = -jnp.einsum("kp,pjw->kjw", sine_table, values, precision=exact_mode)
    twist_cos, twist_sin = phases(
        jnp.arange(2 * seq_parts, dtype=jnp.int32),
        jnp.arange(slot_rows, dtype=jnp.int32),
        length_all,
    )
    twist_cos = twist_cos[:, :, None]
    twist_sin = twist_sin[:, :, None]
    return jnp.stack(
        [
            real_part * twist_cos + imag_part * twist_sin,
            imag_part * twist_cos - real_part * twist_sin,
        ]
    )


def along(spectra):
    row_count = spectra.shape[2]
    index_rows = jnp.arange(row_count, dtype=jnp.int32)
    cosine, sine_table = phases(index_rows, index_rows, row_count)
    cos_real = jnp.einsum("kn,rnw->rkw", cosine, spectra[0], precision=exact_mode)
    cos_imag = jnp.einsum("kn,rnw->rkw", cosine, spectra[1], precision=exact_mode)
    sin_real = jnp.einsum("kn,rnw->rkw", sine_table, spectra[0], precision=exact_mode)
    sin_imag = jnp.einsum("kn,rnw->rkw", sine_table, spectra[1], precision=exact_mode)
    return jnp.stack([cos_real + sin_imag, cos_imag - sin_real])


def back_along(spectra, length_all):
    row_count = spectra.shape[2]
    coarse = spectra.shape[1]
    index_rows = jnp.arange(row_count, dtype=jnp.int32)
    cosine, sine_table = phases(index_rows, index_rows, row_count)
    cos_real = jnp.einsum("nk,rkw->rnw", cosine, spectra[0], precision=exact_mode)
    cos_imag = jnp.einsum("nk,rkw->rnw", cosine, spectra[1], precision=exact_mode)
    sin_real = jnp.einsum("nk,rkw->rnw", sine_table, spectra[0], precision=exact_mode)
    sin_imag = jnp.einsum("nk,rkw->rnw", sine_table, spectra[1], precision=exact_mode)
    inner_real = cos_real - sin_imag
    inner_imag = cos_imag + sin_real
    twist_cos, twist_sin = phases(jnp.arange(coarse, dtype=jnp.int32), index_rows, length_all)
    twist_cos = twist_cos[:, :, None]
    twist_sin = twist_sin[:, :, None]
    return jnp.stack(
        [
            inner_real * twist_cos - inner_imag * twist_sin,
            inner_imag * twist_cos + inner_real * twist_sin,
        ]
    )


def collapse(spectra, length_all):
    coarse = spectra.shape[1]
    seq_parts = coarse // 2
    cosine, sine_table = phases(
        jnp.arange(seq_parts, dtype=jnp.int32), jnp.arange(coarse, dtype=jnp.int32), coarse
    )
    values = jnp.einsum("nk,kjw->njw", cosine, spectra[0], precision=exact_mode)
    values = values - jnp.einsum("nk,kjw->njw", sine_table, spectra[1], precision=exact_mode)
    return values * (1.0 / length_all)


def paired(left_spec, right_spec):
    real_part = left_spec[0] * right_spec[0] + left_spec[1] * right_spec[1]
    imag_part = left_spec[0] * right_spec[1] - left_spec[1] * right_spec[0]
    return jnp.stack([real_part, imag_part])


def spread(matrix, dp_groups, seq_parts):
    row_count = matrix.shape[0]
    narrow = matrix.shape[1] // (dp_groups * seq_parts)
    return jnp.transpose(matrix.reshape(row_count, dp_groups, seq_parts, narrow), (0, 2, 1, 3))


def per_device(inputs, filters, grad_out):
    row_count = inputs.shape[1]
    channels = inputs.shape[2]
    seq_parts = lax.axis_size("seq")
    dp_groups = lax.axis_size("dp")
    length_all = 2 * seq_parts * row_count
    signal = inputs[0]
    cotangent = grad_out[0]
    whole_filter = lax.all_gather(filters, "dp", axis=1, tiled=True)
    narrow = channels // (dp_groups * seq_parts)
    stacked = jnp.stack(
        [
            spread(signal, dp_groups, seq_parts),
            spread(cotangent, dp_groups, seq_parts),
            spread(whole_filter, dp_groups, seq_parts),
        ],
        axis=2,
    )
    moved_rows = lax.all_to_all(stacked, "seq", split_axis=1, concat_axis=0, tiled=True)
    local_grid = moved_rows.reshape(seq_parts, row_count, 3 * dp_groups * narrow)
    spectra = along(across(local_grid, length_all))
    spectra = spectra.reshape(2, 2 * seq_parts, row_count, 3, dp_groups, narrow)
    input_spec = paired(spectra[:, :, :, 2], spectra[:, :, :, 1])
    filter_spec = paired(spectra[:, :, :, 0], spectra[:, :, :, 1])
    joined = jnp.concatenate([input_spec, filter_spec], axis=3)
    slot_count = joined.shape[3]
    flattened = joined.reshape(2, joined.shape[1], row_count, slot_count * narrow)
    result = collapse(back_along(flattened, length_all), length_all).reshape(
        seq_parts * row_count, slot_count, narrow
    )
    grad_in = result[:, :dp_groups]
    grad_filter = lax.psum_scatter(result[:, dp_groups:], "dp", scatter_dimension=1, tiled=True)
    outgoing = jnp.concatenate([grad_in, grad_filter], axis=1).astype(jnp.bfloat16)
    outgoing = outgoing.reshape(seq_parts * row_count, 1, dp_groups + 1, narrow)
    returned = lax.all_to_all(outgoing, "seq", split_axis=0, concat_axis=1, tiled=True)
    grad_inputs = jnp.transpose(returned[:, :, :dp_groups], (0, 2, 1, 3)).reshape(
        1, row_count, channels
    )
    grad_filters = returned[:, :, dp_groups].reshape(row_count, channels // dp_groups)
    return (grad_inputs, grad_filters)


lanes = 128
tile_rows = 16
group = 4
f32 = jnp.float32
bf16 = jnp.bfloat16


def tables(parts, rows):
    total = 2 * parts * rows
    coarse = np.arange(parts + 1)[:, None, None]
    fine = np.arange(rows)[None, :, None]
    index = np.arange(rows)[None, None, :]
    angle = 2.0 * np.pi / total * (index * (coarse + 2 * parts * fine) % total)
    cosine, sine = np.cos(angle), np.sin(angle)
    forward = np.concatenate(
        [
            np.concatenate([cosine, sine], axis=2),
            np.concatenate([-sine, cosine], axis=2),
        ],
        axis=1,
    )
    weight = np.where((np.arange(parts + 1) % parts) == 0, 1.0, 2.0) / total
    backward = np.transpose(forward, (0, 2, 1)) * weight[:, None, None]

    def two_terms(matrix):
        high = matrix.astype(ml_dtypes.bfloat16)
        low = (matrix - high.astype(np.float64)).astype(ml_dtypes.bfloat16)
        return np.concatenate([high, low], axis=1)

    return two_terms(forward), two_terms(backward)


def spread_dft(values):
    count = len(values)
    if count == 1:
        return [(values[0], None), (values[0], None)]
    even, odd = spread_dft(values[0::2]), spread_dft(values[1::2])
    half = count // 2
    out = [None] * (count + 1)
    out[0] = (even[0][0] + odd[0][0], None)
    out[count] = (even[0][0] - odd[0][0], None)
    for k in range(1, half):
        c, s = math.cos(math.pi * k / count), math.sin(math.pi * k / count)
        real = odd[k][0] * c + odd[k][1] * s
        imag = odd[k][1] * c - odd[k][0] * s
        out[k] = (even[k][0] + real, even[k][1] + imag)
        out[count - k] = (even[k][0] - real, imag - even[k][1])
    out[half] = (even[half][0], -odd[half][0])
    return out


def gather_dft(spectrum):
    count = len(spectrum) - 1
    if count == 1:
        return [spectrum[0][0] + spectrum[1][0]]
    half = count // 2
    even, odd = [None] * (half + 1), [None] * (half + 1)
    even[0] = (spectrum[0][0] + spectrum[count][0], None)
    odd[0] = (spectrum[0][0] - spectrum[count][0], None)
    for k in range(1, half):
        c, s = math.cos(math.pi * k / count), math.sin(math.pi * k / count)
        ar, ai = spectrum[k]
        br, bi = spectrum[count - k]
        even[k] = (ar + br, ai - bi)
        dr, di = ar - br, ai + bi
        odd[k] = (dr * c - di * s, di * c + dr * s)
    even[half] = (spectrum[half][0], None)
    odd[half] = (-spectrum[half][1], None)
    out = [None] * count
    out[0::2] = gather_dft(even)
    out[1::2] = gather_dft(odd)
    return out


def two_terms_of(value):
    high = value.astype(bf16)
    return high, (value - high.astype(f32)).astype(bf16)


def exact_dot(table, k, high, low):
    dot = functools.partial(jnp.dot, preferred_element_type=f32)
    size = table.shape[2]
    if high.shape[1] == lanes:
        four = dot(table[k], jnp.concatenate([high, low], axis=1))
        return four[:size, :lanes] + (four[:size, lanes:] + four[size:, :lanes])
    two = dot(table[k], high)
    return two[:size] + (two[size:] + dot(table[k, :size], low))


def kernel(
    parts,
    x_hbm,
    g_hbm,
    f_hbm,
    fwd_hbm,
    inv_hbm,
    gi_hbm,
    gf_hbm,
    gi_ref,
    gf_ref,
    x_ref,
    g_ref,
    f_ref,
    fwd,
    inv,
    xs,
    gs,
    fs,
    xr,
    gr,
    fr,
    gis,
    gfs,
    gir,
    gfr,
    fg_high,
    fg_low,
    x_high,
    x_low,
    g_spec,
    inner,
    table_sem,
    xs_sem,
    xr_sem,
    gs_sem,
    gr_sem,
    fs_sem,
    fr_sem,
    gis_sem,
    gir_sem,
    gfs_sem,
    gfr_sem,
):
    me_s, me_d = lax.axis_index("seq"), lax.axis_index("dp")
    everyone = 2 * parts
    own = me_d * parts + me_s
    rows = x_ref.shape[0]
    half = rows // 2
    low_half = lax.broadcasted_iota(jnp.int32, (half, lanes), 1) < lanes // 2
    low_tile = lax.broadcasted_iota(jnp.int32, (tile_rows, lanes), 1) < lanes // 2

    def swap(mask, first, second):
        return (
            jnp.where(mask, first, pltpu.roll(second, lanes // 2, 1)),
            jnp.where(mask, pltpu.roll(first, lanes // 2, 1), second),
        )

    def loop(start, stop, body):
        def step(i, carry):
            body(i)
            return carry

        lax.fori_loop(start, stop, step, 0)

    barrier = pltpu.get_barrier_semaphore()
    for ahead in range(parts):
        s = me_s + ahead
        s = jnp.where(s >= parts, s - parts, s)
        for d in (1 - me_d, me_d)[: 2 if ahead else 1]:
            pl.semaphore_signal(
                barrier, inc=1, device_id=(s, d), device_id_type=pl.DeviceIdType.MESH
            )
    f_copy = pltpu.make_async_copy(f_hbm, f_ref, table_sem.at[2])
    g_copy = pltpu.make_async_copy(g_hbm, g_ref, table_sem.at[3])
    x_copy = pltpu.make_async_copy(x_hbm, x_ref, table_sem.at[4])
    fwd_copy = pltpu.make_async_copy(fwd_hbm, fwd, table_sem.at[0])
    inv_copy = pltpu.make_async_copy(inv_hbm, inv, table_sem.at[1])
    f_copy.start()
    g_copy.start()
    x_copy.start()
    fwd_copy.start()
    inv_copy.start()

    def pack_pair(source, target, m):
        column = pl.ds(pl.multiple_of(m * lanes, lanes), lanes)
        first, second = swap(
            low_half,
            source[0:half, column].astype(f32),
            source[half:rows, column].astype(f32),
        )
        target[2 * m] = first.astype(bf16)
        target[2 * m + 1] = second.astype(bf16)

    def pack(source, target):
        loop(0, source.shape[1] // lanes, functools.partial(pack_pair, source, target))

    def unpack(source, target):
        def step(m):
            column = pl.ds(pl.multiple_of(m * lanes, lanes), lanes)
            first, second = swap(
                low_half, source[2 * m].astype(f32), source[2 * m + 1].astype(f32)
            )
            target[0:half, column] = first.astype(bf16)
            target[half:rows, column] = second.astype(bf16)

        loop(0, target.shape[1] // lanes, step)

    def exchange(source, target, send, receive, mine, device_of):
        count = source.shape[0]

        def start(i):
            pltpu.make_async_remote_copy(
                src_ref=source.at[i],
                dst_ref=target.at[mine],
                send_sem=send.at[0],
                recv_sem=receive.at[0],
                device_id=device_of(i),
                device_id_type=pl.DeviceIdType.MESH,
            ).start()

        def pair(step, before):
            m = lax.div(mine, 2) + step
            m = jnp.where(m >= count // 2, m - count // 2, m)
            if before is not None:
                before(m)
            for i in (2 * m, 2 * m + 1):
                pl.when(i != mine)(functools.partial(start, i))

        def start_all(before=None):
            loop(0, count // 2, lambda step: pair(step, before))
            target[mine] = source[mine]

        others = pl.ds(0, count - 1)
        everything = pltpu.make_async_remote_copy(
            src_ref=source.at[others],
            dst_ref=target.at[others],
            send_sem=send.at[0],
            recv_sem=receive.at[0],
            device_id=device_of(lax.rem(mine + 1, count)),
            device_id_type=pl.DeviceIdType.MESH,
        )
        return start_all, everything.wait_recv, everything.wait_send

    def device_at(i):
        d = jnp.where(i >= parts, 1, 0)
        return i - d * parts, d

    def to_all(*refs):
        return exchange(*refs, own, device_at)

    def to_row(*refs):
        return exchange(*refs, me_s, lambda i: (i, me_d))

    f_start, f_wait, f_sent = to_row(fs, fr, fs_sem, fr_sem)
    g_start, g_wait, g_sent = to_all(gs, gr, gs_sem, gr_sem)
    x_start, x_wait, x_sent = to_all(xs, xr, xs_sem, xr_sem)
    gi_start, gi_wait, gi_sent = to_all(gis, gir, gis_sem, gir_sem)
    gf_start, gf_wait, gf_sent = to_row(gfs, gfr, gfs_sem, gfr_sem)

    f_copy.wait()
    pack(f_ref, fs)
    g_copy.wait()
    x_copy.wait()
    pl.semaphore_wait(barrier, everyone - 1)
    f_start()
    g_start(functools.partial(pack_pair, g_ref, gs))
    x_start(functools.partial(pack_pair, x_ref, xs))

    zeros = jnp.zeros((rows, lanes), bf16)

    def spread_to(load, high, low, lane_at):
        columns = slice(lane_at, lane_at + lanes)
        for k in (0, parts):
            high[k, rows:, columns] = zeros
            low[k, rows:, columns] = zeros

        def step(t):
            at = pl.multiple_of(t * tile_rows, tile_rows)
            for side in range(2):
                values = [load(p, pl.ds(at, tile_rows))[side] for p in range(parts)]
                for k, (real, imag) in enumerate(spread_dft(values)):
                    where = pl.ds(side * half + at, tile_rows)
                    high[k, where, columns], low[k, where, columns] = two_terms_of(real)
                    if imag is not None:
                        where = pl.ds(rows + side * half + at, tile_rows)
                        high[k, where, columns], low[k, where, columns] = two_terms_of(imag)

        loop(0, half // tile_rows, step)

    def load_pair(source):
        def load(p, where):
            return swap(
                low_tile, source[p, where].astype(f32), source[parts + p, where].astype(f32)
            )

        return load

    def load_twice(p, where):
        value = fr[p, where].astype(f32)
        return swap(low_tile, value, value)

    def product(left, right):
        lr, li, rr, ri = left[:rows], left[rows:], right[:rows], right[rows:]
        return two_terms_of(
            jnp.concatenate([lr * rr + li * ri, lr * ri - li * rr], axis=0)
        )

    def in_groups(step):
        loop(0, parts // group, lambda g: step([g * group + j for j in range(group)]))
        step([parts])

    def gather_from(store):
        def step(t):
            at = pl.multiple_of(t * tile_rows, tile_rows)
            found = []
            for side in range(2):
                spectrum = []
                for k in range(parts + 1):
                    real = inner[k, pl.ds(side * half + at, tile_rows)]
                    imag = None
                    if k % parts:
                        imag = inner[k, pl.ds(rows + side * half + at, tile_rows)]
                    spectrum.append((real, imag))
                found.append(gather_dft(spectrum))
            for q in range(parts):
                store(q, pl.ds(at, tile_rows), found[0][q], found[1][q])

        loop(0, half // tile_rows, step)

    f_wait()
    spread_to(load_twice, fg_high, fg_low, 0)
    g_wait()
    spread_to(load_pair(gr), fg_high, fg_low, lanes)
    fwd_copy.wait()
    inv_copy.wait()

    def input_step(ks):
        both = [exact_dot(fwd, k, fg_high[k], fg_low[k]) for k in ks]
        for k, spectrum in zip(ks, both):
            g_spec[k] = spectrum[:, lanes:]
        terms = [product(spectrum[:, :lanes], spectrum[:, lanes:]) for spectrum in both]
        for k, term in zip(ks, terms):
            inner[k] = exact_dot(inv, k, *term)

    in_groups(input_step)

    def store_input(q, where, top, bottom):
        first, second = swap(low_tile, top, bottom)
        gis[q, where] = first.astype(bf16)
        gis[parts + q, where] = second.astype(bf16)

    gather_from(store_input)
    gi_start()

    x_wait()
    spread_to(load_pair(xr), x_high, x_low, 0)

    def filter_step(ks):
        left = [exact_dot(fwd, k, x_high[k], x_low[k]) for k in ks]
        terms = [product(spectrum, g_spec[k]) for k, spectrum in zip(ks, left)]
        for k, term in zip(ks, terms):
            inner[k] = exact_dot(inv, k, *term)

    in_groups(filter_step)

    def store_filter(q, where, top, bottom):
        first, second = swap(low_tile, top, bottom)
        gfs[q, where] = (first + second).astype(bf16)

    gather_from(store_filter)
    gf_start()

    f_sent()
    g_sent()
    x_sent()
    gi_wait()
    unpack(gir, gi_ref)
    gi_copy = pltpu.make_async_copy(gi_ref, gi_hbm, table_sem.at[5])
    gi_copy.start()
    gi_sent()
    gf_wait()
    unpack(gfr, gf_ref)
    gf_copy = pltpu.make_async_copy(gf_ref, gf_hbm, table_sem.at[6])
    gf_copy.start()
    gf_sent()
    gi_copy.wait()
    gf_copy.wait()


def whole_kernel(inputs, filters, grad_out):
    rows, channels = inputs.shape[1], inputs.shape[2]
    parts = lax.axis_size("seq")
    forward, backward = tables(parts, rows)
    half = rows // 2
    every = lambda: pltpu.VMEM((2 * parts, half, lanes), bf16)
    row = lambda: pltpu.VMEM((parts, half, lanes), bf16)
    spec = lambda width, dtype: pltpu.VMEM((parts + 1, 2 * rows, width), dtype)
    sems = lambda count: pltpu.SemaphoreType.DMA((count,))
    hbm = pl.BlockSpec(memory_space=pltpu.HBM)
    grad_in, grad_filter = pl.pallas_call(
        functools.partial(kernel, parts),
        out_shape=(
            jax.ShapeDtypeStruct((rows, channels), bf16),
            jax.ShapeDtypeStruct(filters.shape, bf16),
        ),
        in_specs=[hbm] * 5,
        out_specs=(hbm, hbm),
        scratch_shapes=[
            pltpu.VMEM((rows, channels), bf16),
            pltpu.VMEM(filters.shape, bf16),
            pltpu.VMEM((rows, channels), bf16),
            pltpu.VMEM((rows, channels), bf16),
            pltpu.VMEM(filters.shape, bf16),
            pltpu.VMEM(forward.shape, bf16),
            pltpu.VMEM(backward.shape, bf16),
            every(),
            every(),
            row(),
            every(),
            every(),
            row(),
            every(),
            row(),
            every(),
            row(),
            spec(2 * lanes, bf16),
            spec(2 * lanes, bf16),
            spec(lanes, bf16),
            spec(lanes, bf16),
            spec(lanes, f32),
            spec(lanes, f32),
            sems(7),
            *[sems(1) for _ in range(10)],
        ],
        compiler_params=pltpu.CompilerParams(
            collective_id=0, has_side_effects=True, vmem_limit_bytes=60 * 2**20
        ),
    )(inputs[0], grad_out[0], filters, jnp.asarray(forward), jnp.asarray(backward))
    return grad_in[None], grad_filter


def choose(inputs, filters, grad_out):
    rows, channels = inputs.shape[1], inputs.shape[2]
    parts, groups = lax.axis_size("seq"), lax.axis_size("dp")
    fits = (
        groups == 2
        and channels == lanes // 2 * groups * parts
        and rows % (2 * tile_rows) == 0
        and parts % group == 0
        and parts <= 16
        and rows <= 128
    )
    return (whole_kernel if fits else per_device)(inputs, filters, grad_out)


def solution(mesh):
    return jax.shard_map(
        choose,
        mesh=mesh,
        in_specs=(P("dp", "seq", None), P("seq", "dp"), P("dp", "seq", None)),
        out_specs=(P("dp", "seq", None), P("seq", "dp")),
        check_vma=False,
    )
```
